256 devices in a mesh: cam: 16 (over y, x), blk: 16 (over z, core).
Axes of the slice: x: 4, y: 4, z: 8, core: 2. Of those that a mesh axis runs over, the one named last changes fastest.
Arguments:
- cam_index: int32 [16, 16, 2, 16, 128], P('cam', 'blk'), may hold values from 0 to 64, as said below
- point_index: int32 [16, 16, 2, 16, 128], P('cam', 'blk'), may hold values from 0 to 31
- jac_cam: float32 [16, 16, 2, 12, 16, 128], P('cam', 'blk'), may hold values from -12 to 12
- jac_point: float32 [16, 16, 2, 6, 16, 128], P('cam', 'blk'), may hold values from -0.9 to 0.9
- point_damping: float32 [16, 16, 32], P('cam', 'blk'), may hold values from 0.1 to 1
Outputs:
- schur_band: float32 [98304, 6144], P(('cam', 'blk'))
The draws below stay inside these ranges and needn't reach their ends.
Inputs may be any that keep to these rules, and one draw needn't show every extreme that they name: `cam_index`: 64 marks an empty slot; every slot with p = 1 in the bands of the last segment is empty.
All inputs are finite; a program needn't handle non-finite values.
Results may differ from the reference program's by a relative error of at most 0.0034.
Values may be sent and summed in bfloat16 or wider, within the bound.
No kernel may reach another device: no remote copies, remote signals or barrier semaphores. Data moves between devices by JAX's collectives and lax.ppermute only.
A program may use at most 256 MiB of HBM per device.

```python
import math
import jax
import jax.numpy as jnp
from jax import lax

NCAM = 64
PTS_BLK = 32
SLOTS = 128
SEGS = 16
N_BLK = 16


def draw_cam_index(key, part):
    key = jax.random.fold_in(key, 11)
    key_cams, key_empty = jax.random.split(key)
    shape = (SEGS, N_BLK, 2, N_BLK, SLOTS)
    cameras = jax.random.randint(key_cams, shape, 0, NCAM)
    empty = jax.random.randint(key_empty, shape, 0, 4) == 0
    seg_ids = lax.broadcasted_iota(jnp.int32, shape, 0)
    part_ids = lax.broadcasted_iota(jnp.int32, shape, 2)
    last = (seg_ids == SEGS - 1) & (part_ids == 1)
    return jnp.where(empty | last, NCAM, cameras).astype(jnp.int32)


def with_ends(values, stream_key, least, top_value):
    spot = [jax.random.randint(jax.random.fold_in(stream_key, axis), (), 0, length) for axis, length in enumerate(values.shape)]
    main_axis = values.shape.index(max(values.shape))
    beside = spot[:main_axis] + [(spot[main_axis] + 1) % values.shape[main_axis]] + spot[main_axis + 1:]
    return values.at[tuple(spot)].set(least).at[tuple(beside)].set(top_value)


def steps_of(rng, shape, cuts, low, top_value):
    def one(dim, parts):
        draws = jax.random.uniform(jax.random.fold_in(jax.random.fold_in(rng, 6), dim), (parts,), jnp.float32, low / len(cuts), top_value / len(cuts))
        return jnp.repeat(jnp.exp(draws), shape[dim] // parts).reshape((-1,) + (1,) * (len(shape) - dim - 1))

    gain = one(*cuts[0])
    for cut in cuts[1:]:
        gain = gain * one(*cut)
    return gain


def bell_draw(own_key, shape, scale, bound, pieces=(), kind=jnp.bfloat16):
    values = scale * jax.random.normal(own_key, shape, jnp.float32)
    if pieces:
        values = values * steps_of(own_key, shape, pieces, -0.22, 0.18)
    return jnp.clip(values, -bound, bound).astype(kind)


def setup_inputs(seed: int = 0) -> dict:
    key_of = jax.random.split(jax.random.key(seed), 6)
    cam_index = draw_cam_index(jax.random.fold_in(key_of[5], 71), 0)
    point_index = with_ends(jax.random.randint(key_of[1], (SEGS, N_BLK, 2, N_BLK, SLOTS), 0, PTS_BLK), jax.random.fold_in(key_of[1], 1), 0, PTS_BLK - 1).astype(jnp.int32)
    jac_cam = bell_draw(key_of[2], (SEGS, N_BLK, 2, 12, N_BLK, SLOTS), 2.0, 12.0, ((0, 16), (1, 16)), jnp.float32)
    jac_point = bell_draw(key_of[3], (SEGS, N_BLK, 2, 6, N_BLK, SLOTS), 0.15, 0.9, ((0, 16), (1, 16)), jnp.float32)
    point_damping = jnp.clip(jnp.exp(math.log(1.0) - 2.3025851 * jax.random.uniform(key_of[4], (SEGS, N_BLK, PTS_BLK), jnp.float32) ** steps_of(key_of[4], (SEGS, N_BLK, PTS_BLK), ((0, 16), (1, 16)), -0.2, 0.2)), 0.1, 1.0)
    return dict(cam_index=cam_index, point_index=point_index, jac_cam=jac_cam, jac_point=jac_point, point_damping=point_damping)


PAIRS = ((0, 0), (0, 1), (0, 2), (1, 1), (1, 2), (2, 2))
DIAG_MASK = (1.0, 0.0, 0.0, 1.0, 0.0, 1.0)

def products(tracks):
    return jnp.stack([tracks[band_position] * tracks[j] + tracks[3 + band_position] * tracks[3 + j] for band_position, j in PAIRS])

def factor(sym):
    root_first = jnp.sqrt(sym[0])
    low_second = sym[1] / root_first
    low_third = sym[2] / root_first
    root_second = jnp.sqrt(sym[3] - low_second * low_second)
    low_mixed = (sym[4] - low_third * low_second) / root_second
    root_third = jnp.sqrt(sym[5] - low_third * low_third - low_mixed * low_mixed)
    inv_first = 1.0 / root_first
    inv_second = 1.0 / root_second
    inv_third = 1.0 / root_third
    inv_lower = -inv_second * low_second * inv_first
    inv_mixed = -inv_third * low_mixed * inv_second
    inv_corner = -(inv_mixed * low_second + inv_third * low_third) * inv_first
    return jnp.stack([inv_first, inv_lower, inv_second, inv_corner, inv_mixed, inv_third])

def eliminate_points(tracks, looked):
    rows = []
    for row in range(2):
        first = tracks[3 * row]
        second = tracks[3 * row + 1]
        third = tracks[3 * row + 2]
        rows.append(first * looked[0])
        rows.append(first * looked[1] + second * looked[2])
        rows.append(first * looked[3] + second * looked[4] + third * looked[5])
    return jnp.stack(rows)

def contribution_list(camera_row_block, eliminated_tile):
    return jnp.stack([camera_row_block[offset_step] * eliminated_tile[band_position] + camera_row_block[6 + offset_step] * eliminated_tile[3 + band_position] for offset_step in range(6) for band_position in range(3)])

def build_panel(values, bins, width):
    summed = jax.ops.segment_sum(values.T, bins, num_segments=NCAM * width)
    return summed.reshape(NCAM, width, 6, 3).transpose(0, 2, 3, 1).reshape(NCAM * 6, 3 * width).astype(jnp.bfloat16)

def reference(cam_index, point_index, jac_cam, jac_point, point_damping):
    segs = cam_index.shape[0]
    nblk = cam_index.shape[1]
    npts = point_damping.shape[2]
    shape = cam_index.shape
    live = (cam_index < NCAM).astype(jnp.float32)
    camera_row_block = jnp.moveaxis(jac_cam, 3, 0) * live
    tracks = jnp.moveaxis(jac_point, 3, 0) * live
    seg_ids = lax.broadcasted_iota(jnp.int32, shape, 0)
    part_ids = lax.broadcasted_iota(jnp.int32, shape, 2)
    block_ids = lax.broadcasted_iota(jnp.int32, shape, 3)
    total = segs * nblk * npts
    point_ids = ((seg_ids + part_ids) * nblk + block_ids) * npts + point_index
    flat_ids = jnp.minimum(point_ids, total - 1).reshape(-1).astype(jnp.int32)
    sums = jax.ops.segment_sum(products(tracks).reshape(6, -1).T, flat_ids, num_segments=total).T
    sums = sums + point_damping.reshape(-1)[None, :] * jnp.array(DIAG_MASK, jnp.float32)[:, None]
    lookup_table = factor(sums)
    looked = lookup_table[:, flat_ids].reshape(tracks.shape)
    schur_contribution = contribution_list(camera_row_block, eliminate_points(tracks, looked))
    width = 2 * nblk * npts
    bins = ((cam_index * 2 + part_ids) * nblk + block_ids) * npts + point_index
    bins = jnp.minimum(bins, NCAM * width - 1).astype(jnp.int32)

    def one_segment(items):
        contrib_seg, bins_seg = items

        def one_band(values, places):
            return build_panel(values.reshape(18, -1), places.reshape(-1), width)
        panels = jax.vmap(one_band, in_axes=(1, 0))(contrib_seg, bins_seg).astype(jnp.float32)
        tiles = jnp.einsum('brc,dsc->brds', panels, panels)
        return tiles.reshape(nblk * NCAM * 6, nblk * NCAM * 6)
    bands = lax.map(one_segment, (jnp.moveaxis(schur_contribution, 1, 0), bins))
    return bands.reshape(segs * nblk * NCAM * 6, nblk * NCAM * 6)
```

```python
import functools

import jax
import jax.numpy as jnp
from jax import lax
from jax.experimental import pallas as pl
from jax.experimental.pallas import tpu as pltpu
from jax.sharding import PartitionSpec as P

F32 = jnp.float32
BF16 = jnp.bfloat16
NT = (((1,), (1,)), ((), ()))
NCAM = 64
NBLK = 16
PTS = 32
Q = 2 * NBLK
ROWS = NCAM * 6
DEPTH = 3 * PTS * Q
VALS = 26
PAIRS = ((0, 0), (0, 1), (0, 2), (1, 1), (1, 2), (2, 2))


def vmem():
    return pl.BlockSpec(memory_space=pltpu.VMEM)


def smem():
    return pl.BlockSpec(memory_space=pltpu.SMEM)


def params():
    return pltpu.CompilerParams(vmem_limit_bytes=56 * 2**20)


def split(x):
    hi = x.astype(BF16).astype(F32)
    return hi, x - hi


def prepare(ids, cam, pt, jac_cam, jac_point, damping, payload, mine, other, prods):
    core = lax.rem(ids[0], 2)
    lane = lax.broadcasted_iota(jnp.int32, (8, 128), 1)
    entry = lax.broadcasted_iota(jnp.int32, (8, 128), 0)
    diag = (entry == 0) | (entry == 3) | (entry == 5)
    damp = jnp.broadcast_to(jnp.concatenate([damping[...]] * 4, axis=1), (8, 128))
    damp = jnp.where(diag & (lane // PTS == lax.rem(ids[0], 4)), damp, 0.0)
    rows128 = lax.broadcasted_iota(jnp.int32, (128, 128), 0)
    totals = []
    for p in range(2):
        span = pl.ds(p * NBLK, NBLK)
        cams = cam[span]
        live = (cams < NCAM).astype(F32)
        payload[24, span] = cams.astype(F32).astype(BF16)
        payload[25, span] = pt[span].astype(F32).astype(BF16)
        for v in range(12):
            payload[v, span] = jac_cam[p, v].astype(BF16)
        tracks = [jac_point[p, v] * live for v in range(6)]
        for v in range(6):
            hi, lo = split(tracks[v])
            payload[12 + v, span] = hi.astype(BF16)
            payload[18 + v, span] = lo.astype(BF16)
        for e, (i, j) in enumerate(PAIRS):
            prods[span, e] = tracks[i] * tracks[j] + tracks[3 + i] * tracks[3 + j]
        prods[span, 6] = jnp.zeros((NBLK, 128), F32)
        prods[span, 7] = jnp.zeros((NBLK, 128), F32)
        for g in range(4):
            left = []
            right = []
            for t in range(4):
                q = p * NBLK + 4 * g + t
                hi, rest = split(prods[q])
                mid, low = split(rest)
                left.append(jnp.concatenate([hi, mid, low, jnp.zeros((8, 128), F32)], axis=0).astype(BF16))
                spot = jnp.broadcast_to(pt[pl.ds(q, 1)], (128, 128)) + PTS * t
                right.append(jnp.where(spot == rows128, 1.0, 0.0).astype(BF16))
            got = lax.dot_general(
                jnp.concatenate(left, axis=1), jnp.concatenate(right, axis=1), NT, preferred_element_type=F32
            )
            total = got[0:8] + got[8:16] + got[16:24]
            if p == 0:
                total = total + jnp.where(ids[0] // 4 == g, damp, 0.0)
            totals.append(total)
    for g in range(4):
        mine[g] = jnp.where(core == 0, totals[g], totals[4 + g])
        other[g] = jnp.where(core == 0, totals[4 + g], totals[g])


def factor(parts, inverse):
    total = parts[0]
    for n in range(1, 16):
        total = total + parts[n]
    sym = [total[:, e, :] for e in range(6)]
    root_first = jnp.sqrt(sym[0])
    low_second = sym[1] / root_first
    low_third = sym[2] / root_first
    root_second = jnp.sqrt(sym[3] - low_second * low_second)
    low_mixed = (sym[4] - low_third * low_second) / root_second
    root_third = jnp.sqrt(sym[5] - low_third * low_third - low_mixed * low_mixed)
    inv_first = 1.0 / root_first
    inv_second = 1.0 / root_second
    inv_third = 1.0 / root_third
    inv_lower = -inv_second * low_second * inv_first
    inv_mixed = -inv_third * low_mixed * inv_second
    inv_corner = -(inv_mixed * low_second + inv_third * low_third) * inv_first
    for e, x in enumerate((inv_first, inv_lower, inv_second, inv_corner, inv_mixed, inv_third)):
        inverse[e] = x


def eliminate(tracks, spots, table, rows_out):
    offset = lax.rem(lax.broadcasted_iota(jnp.int32, (Q, 128), 0), 4) * PTS
    where = spots + offset
    looked = [jnp.take_along_axis(table[e], where, axis=1) for e in range(6)]
    for r in range(2):
        first, second, third = tracks[3 * r : 3 * r + 3]
        rows_out[3 * r] = first * looked[0]
        rows_out[3 * r + 1] = first * looked[1] + second * looked[2]
        rows_out[3 * r + 2] = first * looked[3] + second * looked[4] + third * looked[5]


def hot(spot, count):
    rows = lax.broadcasted_iota(jnp.int32, (count, 128), 0).astype(F32)
    return jnp.where(jnp.broadcast_to(spot, (count, 128)) == rows, 1.0, 0.0).astype(BF16)


def spread(row, mask):
    value = jnp.broadcast_to(row, (16, 128)).astype(BF16)
    return jnp.concatenate([value] * (mask.shape[0] // 16), axis=0) * mask


def relayout(tile, store):
    low = lax.broadcasted_iota(jnp.int32, (PTS, 128), 1) < NCAM
    for m in range(3):
        even = tile[64 * m : 64 * m + 32]
        odd = tile[64 * m + 32 : 64 * m + 64]
        even_rolled = pltpu.roll(even[:, :128], 64, axis=1)
        odd_rolled = pltpu.roll(odd[:, :128], 64, axis=1)
        store(0, m, jnp.where(low, even[:, :128], odd_rolled))
        store(1, m, jnp.where(low, even_rolled, odd[:, :128]))
        store(2, m, jnp.where(low, even[:, 128:], odd[:, 128:]))


def own_panel(ids, cam, pt, jac_cam, jac_point, inv_mine, inv_other, panel, table, rows_e, rows_j, rows_c, rows_p, turned):
    core = lax.rem(ids[0], 2)
    for e in range(6):
        near, far = inv_mine[e], inv_other[e]
        first = jnp.where(core == 0, near, far)
        second = jnp.where(core == 0, far, near)
        pieces = []
        for half in (first, second):
            for g in range(4):
                pieces.append(jnp.broadcast_to(half[g : g + 1], (4, 128)))
        table[e] = jnp.concatenate(pieces, axis=0)
    cams = cam[...]
    live = (cams < NCAM).astype(F32)
    tracks = [jnp.concatenate([jac_point[0, v], jac_point[1, v]], axis=0) * live for v in range(6)]
    spots = pt[...]
    eliminate(tracks, spots, table, rows_e)
    rows_c[...] = cams.astype(F32)
    rows_p[...] = spots.astype(F32)
    for v in range(12):
        rows_j[v] = jnp.concatenate([jac_cam[0, v], jac_cam[1, v]], axis=0)

    def block(q, carry):
        here = pl.ds(q, 1)
        hot_c = hot(rows_c[here], NCAM)
        hot_p = hot(rows_p[here], PTS)
        left = {}
        right = {}
        for r in range(2):
            hi_k, lo_k, hi_i, lo_i = [], [], [], []
            for k in range(6):
                hi, lo = split(rows_j[6 * r + k, here])
                hi_k.append(spread(hi, hot_p))
                lo_k.append(spread(lo, hot_p))
            for i in (0, 1, 2, 2):
                hi, lo = split(rows_e[3 * r + i, here])
                hi_i.append(spread(hi, hot_c))
                lo_i.append(spread(lo, hot_c))
            left[r] = (jnp.concatenate(hi_k, axis=0), jnp.concatenate(lo_k, axis=0))
            right[r] = (jnp.concatenate(hi_i, axis=0), jnp.concatenate(lo_i, axis=0))
        lhs = jnp.concatenate([left[0][0], left[1][0], left[0][1], left[1][1], left[0][0], left[1][0]], axis=1)
        rhs = jnp.concatenate([right[0][0], right[1][0], right[0][0], right[1][0], right[0][1], right[1][1]], axis=1)
        tile = lax.dot_general(lhs, rhs, NT, preferred_element_type=F32)

        def store(i, m, value):
            at = pl.multiple_of(q * 96 + 32 * i, 32)
            turned[pl.ds(at, 32), 128 * m : 128 * m + 128] = value.astype(BF16)

        relayout(tile, store)
        return carry

    lax.fori_loop(0, Q, block, 0, unroll=2)
    row = lax.broadcasted_iota(jnp.int32, (ROWS, ROWS), 0)
    col = lax.broadcasted_iota(jnp.int32, (ROWS, ROWS), 1)
    order = jnp.where((row // 6 == lax.rem(col, NCAM)) & (lax.rem(row, 6) == col // NCAM), 1.0, 0.0).astype(BF16)
    panel[...] = lax.dot_general(order, turned[...], NT, preferred_element_type=F32).astype(BF16)


def tiles_kernel(n, first, *refs):
    ids = refs[0]
    payloads = refs[1 : 1 + n]
    table, panel = refs[1 + n : 3 + n]
    rest = refs[3 + n :]
    if not first:
        rest = rest[1:]
    out, rows_e, rows_j, rows_c, rows_p, turned, product, shown, sems = rest
    core = lax.rem(ids[0], 2)
    lane = lax.broadcasted_iota(jnp.int32, (8, 128), 1)
    sources = []
    picks = []
    for m in range(3):
        at = 128 * m + lane
        source = lax.rem(at, 6) * NCAM + at // 6
        sources.append(lax.rem(source, 128))
        picks.append(source // 128)

    def copy(t, j):
        column = ids[1 + t] * (2 * ROWS) + ROWS * lax.rem(core + j, 2)
        target = out.at[:, pl.ds(pl.multiple_of(column, 128), ROWS)]
        return pltpu.make_async_copy(shown.at[t % 2, j], target, sems.at[t % 2, j])

    for t in range(n):
        payload = payloads[t]
        for j in range(2):
            spots = payload[j, 25].astype(F32)
            tracks = [payload[j, 12 + v].astype(F32) + payload[j, 18 + v].astype(F32) for v in range(6)]
            eliminate(tracks, spots.astype(jnp.int32), table, rows_e)
            rows_c[...] = payload[j, 24].astype(F32)
            rows_p[...] = spots
            for v in range(12):
                rows_j[v] = payload[j, v].astype(F32)

            def block(q, carry):
                here = pl.ds(q, 1)
                hot_c = hot(rows_c[here], NCAM)
                hot_p = hot(rows_p[here], PTS)
                left = []
                right = []
                for r in range(2):
                    left.append(jnp.concatenate([spread(rows_j[6 * r + k, here], hot_p) for k in range(6)], axis=0))
                    cols = [spread(rows_e[3 * r + i, here], hot_c) for i in range(3)]
                    right.append(jnp.concatenate(cols + [cols[2]], axis=0))
                tile = lax.dot_general(
                    jnp.concatenate(left, axis=1), jnp.concatenate(right, axis=1), NT, preferred_element_type=F32
                )

                def store(i, m, value):
                    at = pl.multiple_of(q * 96 + 32 * i, 32)
                    turned[pl.ds(at, 32), ROWS * j + 128 * m : ROWS * j + 128 * m + 128] = value.astype(BF16)

                relayout(tile, store)
                return carry

            lax.fori_loop(0, Q, block, 0, unroll=8)
        product[...] = jnp.dot(panel[...], turned[...], preferred_element_type=F32)
        if t >= 2:
            for j in range(2):
                copy(t - 2, j).wait()

        def reorder(g, carry):
            rows = pl.ds(pl.multiple_of(g * 8, 8), 8)
            for j in range(2):
                got = [product[rows, ROWS * j + 128 * s : ROWS * j + 128 * s + 128] for s in range(3)]
                for m in range(3):
                    moved = [jnp.take_along_axis(x, sources[m], axis=1) for x in got]
                    value = jnp.where(picks[m] == 0, moved[0], jnp.where(picks[m] == 1, moved[1], moved[2]))
                    shown[t % 2, j, rows, 128 * m : 128 * m + 128] = value
            return carry

        lax.fori_loop(0, ROWS // 8, reorder, 0, unroll=8)
        for j in range(2):
            copy(t, j).start()
    for t in range(max(0, n - 2), n):
        for j in range(2):
            copy(t, j).wait()


def tiles(ids, payloads, table, panel, out):
    n = len(payloads)
    first = out is None
    specs = [smem()] + [vmem()] * (n + 2)
    args = [ids, *payloads, table, panel]
    aliases = {}
    if not first:
        specs.append(pl.BlockSpec(memory_space=pl.ANY))
        args.append(out)
        aliases = {len(args) - 1: 0}
    return pl.pallas_call(
        functools.partial(tiles_kernel, n, first),
        out_shape=jax.ShapeDtypeStruct((ROWS, NBLK * ROWS), F32),
        in_specs=specs,
        out_specs=pl.BlockSpec(memory_space=pl.ANY),
        input_output_aliases=aliases,
        scratch_shapes=[
            pltpu.VMEM((6, Q, 128), F32),
            pltpu.VMEM((12, Q, 128), F32),
            pltpu.VMEM((Q, 128), F32),
            pltpu.VMEM((Q, 128), F32),
            pltpu.VMEM((DEPTH, 2 * ROWS), BF16),
            pltpu.VMEM((ROWS, 2 * ROWS), F32),
            pltpu.VMEM((2, 2, ROWS, ROWS), F32),
            pltpu.SemaphoreType.DMA((2, 2)),
        ],
        compiler_params=params(),
    )(*args)


def body(cam_index, point_index, jac_cam, jac_point, point_damping):
    cam = cam_index.reshape(Q, 128)
    pt = point_index.reshape(Q, 128)
    jac_cam = jac_cam.reshape(2, 12, NBLK, 128)
    jac_point = jac_point.reshape(2, 6, NBLK, 128)
    damping = point_damping.reshape(1, PTS)
    here = lax.axis_index("blk")
    chip = here // 2
    swap = [(n, n ^ 1) for n in range(NBLK)]

    def ids(*steps):
        return jnp.stack([here] + [lax.rem(chip + 8 - s, 8) for s in steps]).astype(jnp.int32)

    only = ids()
    shape = jax.ShapeDtypeStruct
    payload, mine, other = pl.pallas_call(
        prepare,
        out_shape=(shape((VALS, Q, 128), BF16), shape((4, 8, 128), F32), shape((4, 8, 128), F32)),
        in_specs=[smem()] + [vmem()] * 5,
        out_specs=(vmem(),) * 3,
        scratch_shapes=[pltpu.VMEM((Q, 8, 128), F32)],
        compiler_params=params(),
    )(only, cam, pt, jac_cam, jac_point, damping)
    pair_sum = mine + lax.ppermute(other, "blk", swap)
    local = jnp.stack([payload, lax.ppermute(payload, "blk", swap)])
    ups = [local]
    downs = [local]
    up_pairs = [(n, (n + 2) % NBLK) for n in range(NBLK)]
    down_pairs = [(n, (n - 2) % NBLK) for n in range(NBLK)]
    for step in range(4):
        ups.append(lax.ppermute(ups[-1], "blk", up_pairs))
        if step < 3:
            downs.append(lax.ppermute(downs[-1], "blk", down_pairs))
    groups = []
    for s in range(16):
        after = (s + 1) % 16
        groups.append([s * NBLK + 2 * z + 1 for z in range(8)] + [after * NBLK + 2 * z for z in range(8)])
    parts = lax.all_to_all(
        jnp.broadcast_to(pair_sum[None], (16, 4, 8, 128)),
        ("cam", "blk"),
        split_axis=0,
        concat_axis=0,
        axis_index_groups=groups,
        tiled=True,
    )
    inverse = pl.pallas_call(
        factor,
        out_shape=shape((6, 4, 128), F32),
        in_specs=[vmem()],
        out_specs=vmem(),
        compiler_params=params(),
    )(parts)
    inverse_other = lax.ppermute(inverse, "blk", swap)
    panel, table = pl.pallas_call(
        own_panel,
        out_shape=(shape((ROWS, DEPTH), BF16), shape((6, Q, 128), F32)),
        in_specs=[smem()] + [vmem()] * 6,
        out_specs=(vmem(),) * 2,
        scratch_shapes=[
            pltpu.VMEM((6, Q, 128), F32),
            pltpu.VMEM((12, Q, 128), F32),
            pltpu.VMEM((Q, 128), F32),
            pltpu.VMEM((Q, 128), F32),
            pltpu.VMEM((DEPTH, ROWS), BF16),
        ],
        compiler_params=params(),
    )(only, cam, pt, jac_cam, jac_point, inverse, inverse_other)
    out = tiles(ids(0), [local], table, panel, None)
    out = tiles(ids(1, -1), [ups[1], downs[1]], table, panel, out)
    out = tiles(ids(2, -2), [ups[2], downs[2]], table, panel, out)
    out = tiles(ids(3, -3, 4), [ups[3], downs[3], ups[4]], table, panel, out)
    return out


def solution(mesh):
    return jax.shard_map(
        body,
        mesh=mesh,
        in_specs=(
            P("cam", "blk", None, None, None),
            P("cam", "blk", None, None, None),
            P("cam", "blk", None, None, None, None),
            P("cam", "blk", None, None, None, None),
            P("cam", "blk", None),
        ),
        out_specs=P(("cam", "blk"), None),
        check_vma=False,
    )
```

```python
import functools

import jax
import jax.numpy as jnp
import numpy as np
from jax import lax
from jax.experimental import pallas as pl
from jax.experimental.pallas import tpu as pltpu
from jax.sharding import PartitionSpec as P

F32 = jnp.float32
BF16 = jnp.bfloat16
NT = (((1,), (1,)), ((), ()))
NCAM = 64
NBLK = 16
PTS = 32
Q = 2 * NBLK
ROWS = NCAM * 6
DEPTH = 3 * PTS * Q
VALS = 26
PAIRS = ((0, 0), (0, 1), (0, 2), (1, 1), (1, 2), (2, 2))


def vmem():
    return pl.BlockSpec(memory_space=pltpu.VMEM)


def anywhere():
    return pl.BlockSpec(memory_space=pl.ANY)


def smem():
    return pl.BlockSpec(memory_space=pltpu.SMEM)


def params():
    return pltpu.CompilerParams(vmem_limit_bytes=56 * 2**20)


def split(x):
    hi = x.astype(BF16).astype(F32)
    return hi, x - hi


def prepare(ids, cam, pt, jac_cam, jac_point, damping, payload, mine, other, prods):
    core = lax.rem(ids[0], 2)
    lane = lax.broadcasted_iota(jnp.int32, (8, 128), 1)
    entry = lax.broadcasted_iota(jnp.int32, (8, 128), 0)
    diag = (entry == 0) | (entry == 3) | (entry == 5)
    damp = jnp.broadcast_to(jnp.concatenate([damping[...]] * 4, axis=1), (8, 128))
    damp = jnp.where(diag & (lane // PTS == lax.rem(ids[0], 4)), damp, 0.0)
    rows128 = lax.broadcasted_iota(jnp.int32, (128, 128), 0)
    totals = []
    for p in range(2):
        span = pl.ds(p * NBLK, NBLK)
        cams = cam[span]
        live = (cams < NCAM).astype(F32)
        payload[24, span] = cams.astype(F32).astype(BF16)
        payload[25, span] = pt[span].astype(F32).astype(BF16)
        for v in range(12):
            payload[v, span] = jac_cam[p, v].astype(BF16)
        tracks = [jac_point[p, v] * live for v in range(6)]
        for v in range(6):
            hi, lo = split(tracks[v])
            payload[12 + v, span] = hi.astype(BF16)
            payload[18 + v, span] = lo.astype(BF16)
        for e, (i, j) in enumerate(PAIRS):
            prods[span, e] = tracks[i] * tracks[j] + tracks[3 + i] * tracks[3 + j]
        prods[span, 6] = jnp.zeros((NBLK, 128), F32)
        prods[span, 7] = jnp.zeros((NBLK, 128), F32)
        for g in range(4):
            left = []
            right = []
            for t in range(4):
                q = p * NBLK + 4 * g + t
                hi, rest = split(prods[q])
                mid, low = split(rest)
                left.append(jnp.concatenate([hi, mid, low, jnp.zeros((8, 128), F32)], axis=0).astype(BF16))
                spot = jnp.broadcast_to(pt[pl.ds(q, 1)], (128, 128)) + PTS * t
                right.append(jnp.where(spot == rows128, 1.0, 0.0).astype(BF16))
            got = lax.dot_general(
                jnp.concatenate(left, axis=1), jnp.concatenate(right, axis=1), NT, preferred_element_type=F32
            )
            total = got[0:8] + got[8:16] + got[16:24]
            if p == 0:
                total = total + jnp.where(ids[0] // 4 == g, damp, 0.0)
            totals.append(total)
    for g in range(4):
        near = jnp.where(core == 0, totals[g], totals[4 + g])
        far = jnp.where(core == 0, totals[4 + g], totals[g])
        for e in range(6):
            mine[4 * e + g : 4 * e + g + 1] = near[e : e + 1]
            other[4 * e + g : 4 * e + g + 1] = far[e : e + 1]


def invert(total):
    sym = [total[4 * e : 4 * e + 4] for e in range(6)]
    root_first = jnp.sqrt(sym[0])
    low_second = sym[1] / root_first
    low_third = sym[2] / root_first
    root_second = jnp.sqrt(sym[3] - low_second * low_second)
    low_mixed = (sym[4] - low_third * low_second) / root_second
    root_third = jnp.sqrt(sym[5] - low_third * low_third - low_mixed * low_mixed)
    inv_first = 1.0 / root_first
    inv_second = 1.0 / root_second
    inv_third = 1.0 / root_third
    inv_lower = -inv_second * low_second * inv_first
    inv_mixed = -inv_third * low_mixed * inv_second
    inv_corner = -(inv_mixed * low_second + inv_third * low_third) * inv_first
    return (inv_first, inv_lower, inv_second, inv_corner, inv_mixed, inv_third)


def eliminate(tracks, spots, table, rows_out):
    offset = lax.rem(lax.broadcasted_iota(jnp.int32, (Q, 128), 0), 4) * PTS
    where = spots + offset
    looked = [jnp.take_along_axis(table[e], where, axis=1) for e in range(6)]
    for r in range(2):
        first, second, third = tracks[3 * r : 3 * r + 3]
        rows_out[3 * r] = first * looked[0]
        rows_out[3 * r + 1] = first * looked[1] + second * looked[2]
        rows_out[3 * r + 2] = first * looked[3] + second * looked[4] + third * looked[5]


def hot(spot, count):
    rows = lax.broadcasted_iota(jnp.int32, (count, 128), 0).astype(F32)
    return jnp.where(jnp.broadcast_to(spot, (count, 128)) == rows, 1.0, 0.0).astype(BF16)


def spread(row, mask):
    value = jnp.broadcast_to(row, (16, 128)).astype(BF16)
    return jnp.concatenate([value] * (mask.shape[0] // 16), axis=0) * mask


def relayout(tile, store):
    low = lax.broadcasted_iota(jnp.int32, (PTS, 128), 1) < NCAM
    for m in range(3):
        even = tile[64 * m : 64 * m + 32]
        odd = tile[64 * m + 32 : 64 * m + 64]
        even_rolled = pltpu.roll(even[:, :128], 64, axis=1)
        odd_rolled = pltpu.roll(odd[:, :128], 64, axis=1)
        last = jnp.concatenate([even[:, 128:], odd[:, 128:]], axis=1)
        store(0, m, jnp.where(low, even[:, :128], odd_rolled))
        store(1, m, jnp.where(low, even_rolled, odd[:, :128]))
        store(2, m, last)


def place(turned, base, q):
    def store(i, m, value):
        at = pl.multiple_of(q * 96 + 32 * i, 32)
        turned[pl.ds(at, 32), base + 128 * m : base + 128 * m + 128] = value.astype(BF16)

    return store


def own_turned(cam, pt, jac_cam, jac_point, table, rows, turned):
    rows_e, rows_j, rows_c, rows_p = rows
    cams = cam[...]
    live = (cams < NCAM).astype(F32)
    tracks = [jnp.concatenate([jac_point[0, v], jac_point[1, v]], axis=0) * live for v in range(6)]
    spots = pt[...]
    eliminate(tracks, spots, table, rows_e)
    rows_c[...] = cams.astype(F32)
    rows_p[...] = spots.astype(F32)
    for v in range(12):
        rows_j[v] = jnp.concatenate([jac_cam[0, v], jac_cam[1, v]], axis=0)

    def block(q, carry):
        here = pl.ds(q, 1)
        hot_c = hot(rows_c[here], NCAM)
        hot_p = hot(rows_p[here], PTS)
        left = {}
        right = {}
        for r in range(2):
            hi_k, lo_k, hi_i, lo_i = [], [], [], []
            for k in range(6):
                hi, lo = split(rows_j[6 * r + k, here])
                hi_k.append(spread(hi, hot_p))
                lo_k.append(spread(lo, hot_p))
            for i in range(3):
                hi, lo = split(rows_e[3 * r + i, here])
                hi_i.append(spread(hi, hot_c))
                lo_i.append(spread(lo, hot_c))
            left[r] = (jnp.concatenate(hi_k, axis=0), jnp.concatenate(lo_k, axis=0))
            right[r] = (jnp.concatenate(hi_i, axis=0), jnp.concatenate(lo_i, axis=0))
        lhs = jnp.concatenate([left[0][0], left[1][0], left[0][1], left[1][1], left[0][0], left[1][0]], axis=1)
        rhs = jnp.concatenate([right[0][0], right[1][0], right[0][0], right[1][0], right[0][1], right[1][1]], axis=1)
        relayout(lax.dot_general(lhs, rhs, NT, preferred_element_type=F32), place(turned, 0, q))
        return carry

    lax.fori_loop(0, Q, block, 0, unroll=32)


def band_turned(payload, table, rows, turned, base):
    rows_e, rows_j, rows_c, rows_p = rows
    spots = payload[25].astype(F32)
    tracks = [payload[12 + v].astype(F32) + payload[18 + v].astype(F32) for v in range(6)]
    eliminate(tracks, spots.astype(jnp.int32), table, rows_e)
    rows_c[...] = payload[24].astype(F32)
    rows_p[...] = spots
    for v in range(12):
        rows_j[v] = payload[v].astype(F32)

    def block(q, carry):
        here = pl.ds(q, 1)
        hot_c = hot(rows_c[here], NCAM)
        hot_p = hot(rows_p[here], PTS)
        left = []
        right = []
        for r in range(2):
            left.append(jnp.concatenate([spread(rows_j[6 * r + k, here], hot_p) for k in range(6)], axis=0))
            cols = [spread(rows_e[3 * r + i, here], hot_c) for i in range(3)]
            right.append(jnp.concatenate(cols, axis=0))
        tile = lax.dot_general(
            jnp.concatenate(left, axis=1), jnp.concatenate(right, axis=1), NT, preferred_element_type=F32
        )
        relayout(tile, place(turned, base, q))
        return carry

    lax.fori_loop(0, Q, block, 0, unroll=32)


def finish(panel, order, turned, product, shown, slot):
    product[...] = jnp.dot(panel[...], turned[...], preferred_element_type=F32)
    for j in range(2):
        got = product[:, ROWS * j : ROWS * (j + 1)]
        hi = got.astype(BF16)
        lo = (got - hi.astype(F32)).astype(BF16)
        both = jnp.concatenate([hi, lo], axis=1)
        shown[slot, j] = lax.dot_general(both, order[...], NT, preferred_element_type=F32)


def out_copy(shown, slot, j, out, column, sems):
    target = out.at[:, pl.ds(pl.multiple_of(column, 128), ROWS)]
    return pltpu.make_async_copy(shown.at[slot, j], target, sems.at[slot, j])


def fetch(refs, sems):
    return [pltpu.make_async_copy(x, y, sems.at[n]) for n, (x, y) in enumerate(refs)]


def first_tiles(
    ids, cam, pt, jac_cam, jac_point, sum_mine, sum_other, order, mate,
    out, panel_out, table, rows_e, rows_j, rows_c, rows_p, turned, product, shown, sems, panel, keep,
):
    rows = (rows_e, rows_j, rows_c, rows_p)
    core = lax.rem(ids[0], 2)
    chip = ids[0] // 2
    near, far = invert(sum_mine[...]), invert(sum_other[...])
    for e in range(6):
        pieces = []
        for half in (jnp.where(core == 0, near[e], far[e]), jnp.where(core == 0, far[e], near[e])):
            for g in range(4):
                pieces.append(jnp.broadcast_to(half[g : g + 1], (4, 128)))
        table[e] = jnp.concatenate(pieces, axis=0)
    own_turned(cam, pt, jac_cam, jac_point, table, rows, turned)
    panel[...] = lax.dot_general(
        order[:, :ROWS], turned[:, :ROWS], NT, preferred_element_type=F32
    ).astype(BF16)
    saved = fetch([(panel, panel_out)], keep)[0]
    saved.start()
    band_turned(mate.at[1], table, rows, turned, ROWS)
    finish(panel, order, turned, product, shown, 0)
    copies = [
        out_copy(shown, 0, j, out, chip * (2 * ROWS) + ROWS * lax.rem(core + j, 2), sems) for j in range(2)
    ]
    for copy in copies:
        copy.start()
    for copy in copies:
        copy.wait()
    saved.wait()


def more_tiles(steps, *refs):
    n = len(steps)
    ids, payloads, (table, order_in, panel_in, _) = refs[0], refs[1 : 1 + n], refs[1 + n : 5 + n]
    out, rows_e, rows_j, rows_c, rows_p, turned, product, shown, sems, panel, keep, order = refs[5 + n :]
    rows = (rows_e, rows_j, rows_c, rows_p)
    core = lax.rem(ids[0], 2)
    chip = ids[0] // 2
    fetched = fetch([(panel_in, panel), (order_in, order)], keep)
    for copy in fetched:
        copy.start()

    def place_out(t, j):
        there = lax.rem(chip + steps[t], 8)
        return out_copy(shown, t % 2, j, out, there * (2 * ROWS) + ROWS * lax.rem(core + j, 2), sems)

    for t in range(n):
        for j in range(2):
            band_turned(payloads[t].at[j], table, rows, turned, ROWS * j)
        if t == 0:
            for copy in fetched:
                copy.wait()
        if t >= 2:
            for j in range(2):
                place_out(t - 2, j).wait()
        finish(panel, order, turned, product, shown, t % 2)
        for j in range(2):
            place_out(t, j).start()
    for t in range(max(0, n - 2), n):
        for j in range(2):
            place_out(t, j).wait()


def more(ids, steps, payloads, table, order, panel, out):
    n = len(payloads)
    return pl.pallas_call(
        functools.partial(more_tiles, steps),
        out_shape=jax.ShapeDtypeStruct(out.shape, out.dtype),
        in_specs=[smem()] + [vmem()] * (n + 1) + [anywhere()] * 3,
        out_specs=anywhere(),
        input_output_aliases={n + 4: 0},
        scratch_shapes=scratch() + [pltpu.VMEM((ROWS, 2 * ROWS), BF16)],
        compiler_params=params(),
    )(ids, *payloads, table, order, panel, out)


def scratch():
    return [
        pltpu.VMEM((6, Q, 128), F32),
        pltpu.VMEM((12, Q, 128), F32),
        pltpu.VMEM((Q, 128), F32),
        pltpu.VMEM((Q, 128), F32),
        pltpu.VMEM((DEPTH, 2 * ROWS), BF16),
        pltpu.VMEM((ROWS, 2 * ROWS), F32),
        pltpu.VMEM((2, 2, ROWS, ROWS), F32),
        pltpu.SemaphoreType.DMA((2, 2)),
        pltpu.VMEM((ROWS, DEPTH), BF16),
        pltpu.SemaphoreType.DMA((2,)),
    ]


def order_matrix():
    row = np.arange(ROWS)
    one = (row[:, None] // 6 == row[None] % NCAM) & (row[:, None] % 6 == row[None] // NCAM)
    return np.concatenate([one, one], axis=1).astype(np.float32)


def body(cam_index, point_index, jac_cam, jac_point, point_damping):
    cam = cam_index.reshape(Q, 128)
    pt = point_index.reshape(Q, 128)
    jac_cam = jac_cam.reshape(2, 12, NBLK, 128)
    jac_point = jac_point.reshape(2, 6, NBLK, 128)
    damping = point_damping.reshape(1, PTS)
    ids = lax.axis_index("blk").astype(jnp.int32).reshape(1)
    order = jnp.asarray(order_matrix(), BF16)
    shape = jax.ShapeDtypeStruct
    payload, mine, other = pl.pallas_call(
        prepare,
        out_shape=(shape((VALS, Q, 128), BF16), shape((24, 128), F32), shape((24, 128), F32)),
        in_specs=[smem()] + [vmem()] * 5,
        out_specs=(vmem(),) * 3,
        scratch_shapes=[pltpu.VMEM((Q, 8, 128), F32)],
        compiler_params=params(),
    )(ids, cam, pt, jac_cam, jac_point, damping)

    def moved(x, by, cross):
        pairs = [(n, (n + 2 * by) % NBLK ^ cross) for n in range(NBLK)]
        return lax.ppermute(x, "blk", pairs)

    parts = mine + moved(other, 0, 1)
    local = jnp.stack([payload, moved(payload, 0, 1)])
    up1, down1 = moved(local, 1, 0), moved(local, -1, 0)
    groups = []
    for s in range(16):
        after = (s + 1) % 16
        groups.append([s * NBLK + 2 * z + 1 for z in range(8)] + [after * NBLK + 2 * z for z in range(8)])
    parts = lax.all_to_all(
        jnp.broadcast_to(parts[None], (16, 24, 128)),
        ("cam", "blk"),
        split_axis=0,
        concat_axis=0,
        axis_index_groups=groups,
        tiled=True,
    )
    sum_mine = parts.sum(axis=0)
    sum_other = moved(sum_mine, 0, 1)
    up1, down1, sum_mine = lax.optimization_barrier((up1, down1, sum_mine))
    sum_other = moved(sum_mine, 0, 1)
    up2, down2 = moved(up1, 1, 0), moved(down1, -1, 0)
    result = shape((ROWS, NBLK * ROWS), F32)
    out, panel, table = pl.pallas_call(
        first_tiles,
        out_shape=(result, shape((ROWS, DEPTH), BF16), shape((6, Q, 128), F32)),
        in_specs=[smem()] + [vmem()] * 8,
        out_specs=(anywhere(), anywhere(), vmem()),
        scratch_shapes=scratch(),
        compiler_params=params(),
    )(ids, cam, pt, jac_cam, jac_point, sum_mine, sum_other, order, local)
    up2, down2, out = lax.optimization_barrier((up2, down2, out))
    up3, down3 = moved(up2, 1, 0), moved(down2, -1, 0)
    out = more(ids, (7, 1), [up1, down1], table, order, panel, out)
    up3, out = lax.optimization_barrier((up3, out))
    up4 = moved(up3, 1, 0)
    out = more(ids, (6, 2), [up2, down2], table, order, panel, out)
    return more(ids, (5, 3, 4), [up3, down3, up4], table, order, panel, out)


def solution(mesh):
    return jax.shard_map(
        body,
        mesh=mesh,
        in_specs=(
            P("cam", "blk", None, None, None),
            P("cam", "blk", None, None, None),
            P("cam", "blk", None, None, None, None),
            P("cam", "blk", None, None, None, None),
            P("cam", "blk", None),
        ),
        out_specs=P(("cam", "blk"), None),
        check_vma=False,
    )
```

```python
import functools

import jax
import jax.numpy as jnp
import numpy as np
from jax import lax
from jax.experimental import pallas as pl
from jax.experimental.pallas import tpu as pltpu
from jax.sharding import PartitionSpec as P

F32 = jnp.float32
BF16 = jnp.bfloat16
NT = (((1,), (1,)), ((), ()))
NCAM = 64
NBLK = 16
PTS = 32
Q = 2 * NBLK
ROWS = NCAM * 6
DEPTH = 3 * PTS * Q
VALS = 26
PAIRS = ((0, 0), (0, 1), (0, 2), (1, 1), (1, 2), (2, 2))


def vmem():
    return pl.BlockSpec(memory_space=pltpu.VMEM)


def anywhere():
    return pl.BlockSpec(memory_space=pl.ANY)


def smem():
    return pl.BlockSpec(memory_space=pltpu.SMEM)


def params():
    return pltpu.CompilerParams(vmem_limit_bytes=62 * 2**20)


def cost(us):
    return pl.CostEstimate(flops=int(us * 1.2e9), transcendentals=0, bytes_accessed=int(us * 3e6))


def split(x):
    hi = x.astype(BF16).astype(F32)
    return hi, x - hi


def prepare(ids, cam, pt, jac_cam, jac_point, damping, payload, mine, other, prods):
    core = lax.rem(ids[0], 2)
    lane = lax.broadcasted_iota(jnp.int32, (8, 128), 1)
    entry = lax.broadcasted_iota(jnp.int32, (8, 128), 0)
    diag = (entry == 0) | (entry == 3) | (entry == 5)
    damp = jnp.broadcast_to(jnp.concatenate([damping[...]] * 4, axis=1), (8, 128))
    damp = jnp.where(diag & (lane // PTS == lax.rem(ids[0], 4)), damp, 0.0)
    rows128 = lax.broadcasted_iota(jnp.int32, (128, 128), 0)
    totals = []
    for p in range(2):
        span = pl.ds(p * NBLK, NBLK)
        cams = cam[span]
        live = (cams < NCAM).astype(F32)
        payload[24, span] = cams.astype(F32).astype(BF16)
        payload[25, span] = pt[span].astype(F32).astype(BF16)
        for v in range(12):
            payload[v, span] = jac_cam[p, v].astype(BF16)
        tracks = [jac_point[p, v] * live for v in range(6)]
        for v in range(6):
            hi, lo = split(tracks[v])
            payload[12 + v, span] = hi.astype(BF16)
            payload[18 + v, span] = lo.astype(BF16)
        for e, (i, j) in enumerate(PAIRS):
            prods[span, e] = tracks[i] * tracks[j] + tracks[3 + i] * tracks[3 + j]
        prods[span, 6] = jnp.zeros((NBLK, 128), F32)
        prods[span, 7] = jnp.zeros((NBLK, 128), F32)
        for g in range(4):
            left = []
            right = []
            for t in range(4):
                q = p * NBLK + 4 * g + t
                hi, rest = split(prods[q])
                mid, low = split(rest)
                left.append(jnp.concatenate([hi, mid, low, jnp.zeros((8, 128), F32)], axis=0).astype(BF16))
                spot = jnp.broadcast_to(pt[pl.ds(q, 1)], (128, 128)) + PTS * t
                right.append(jnp.where(spot == rows128, 1.0, 0.0).astype(BF16))
            got = lax.dot_general(
                jnp.concatenate(left, axis=1), jnp.concatenate(right, axis=1), NT, preferred_element_type=F32
            )
            total = got[0:8] + got[8:16] + got[16:24]
            if p == 0:
                total = total + jnp.where(ids[0] // 4 == g, damp, 0.0)
            totals.append(total)
    for g in range(4):
        near = jnp.where(core == 0, totals[g], totals[4 + g])
        far = jnp.where(core == 0, totals[4 + g], totals[g])
        for e in range(6):
            mine[4 * e + g : 4 * e + g + 1] = near[e : e + 1]
            other[4 * e + g : 4 * e + g + 1] = far[e : e + 1]


def invert(total):
    sym = [total[4 * e : 4 * e + 4] for e in range(6)]
    root_first = jnp.sqrt(sym[0])
    low_second = sym[1] / root_first
    low_third = sym[2] / root_first
    root_second = jnp.sqrt(sym[3] - low_second * low_second)
    low_mixed = (sym[4] - low_third * low_second) / root_second
    root_third = jnp.sqrt(sym[5] - low_third * low_third - low_mixed * low_mixed)
    inv_first = 1.0 / root_first
    inv_second = 1.0 / root_second
    inv_third = 1.0 / root_third
    inv_lower = -inv_second * low_second * inv_first
    inv_mixed = -inv_third * low_mixed * inv_second
    inv_corner = -(inv_mixed * low_second + inv_third * low_third) * inv_first
    return (inv_first, inv_lower, inv_second, inv_corner, inv_mixed, inv_third)


def eliminate(tracks, spots, table, rows_out):
    offset = lax.rem(lax.broadcasted_iota(jnp.int32, (Q, 128), 0), 4) * PTS
    where = spots + offset
    looked = [jnp.take_along_axis(table[e], where, axis=1) for e in range(6)]
    for r in range(2):
        first, second, third = tracks[3 * r : 3 * r + 3]
        rows_out[3 * r] = first * looked[0]
        rows_out[3 * r + 1] = first * looked[1] + second * looked[2]
        rows_out[3 * r + 2] = first * looked[3] + second * looked[4] + third * looked[5]


def hot(spot, count):
    rows = lax.broadcasted_iota(jnp.int32, (count, 128), 0).astype(F32)
    return jnp.where(jnp.broadcast_to(spot, (count, 128)) == rows, 1.0, 0.0).astype(BF16)


def spread(row, mask):
    value = jnp.broadcast_to(row, (16, 128)).astype(BF16)
    return jnp.concatenate([value] * (mask.shape[0] // 16), axis=0) * mask


def relayout(tile, store):
    low = lax.broadcasted_iota(jnp.int32, (PTS, 128), 1) < NCAM
    for m in range(3):
        even = tile[64 * m : 64 * m + 32]
        odd = tile[64 * m + 32 : 64 * m + 64]
        even_rolled = pltpu.roll(even[:, :128], 64, axis=1)
        odd_rolled = pltpu.roll(odd[:, :128], 64, axis=1)
        last = jnp.concatenate([even[:, 128:], odd[:, 128:]], axis=1)
        store(0, m, jnp.where(low, even[:, :128], odd_rolled))
        store(1, m, jnp.where(low, even_rolled, odd[:, :128]))
        store(2, m, last)


def place(turned, base, q):
    def store(i, m, value):
        at = pl.multiple_of(q * 96 + 32 * i, 32)
        turned[pl.ds(at, 32), base + 128 * m : base + 128 * m + 128] = value.astype(BF16)

    return store


def own_turned(cam, pt, jac_cam, jac_point, table, rows, turned):
    rows_e, rows_j, rows_c, rows_p = rows
    cams = cam[...]
    live = (cams < NCAM).astype(F32)
    tracks = [jnp.concatenate([jac_point[0, v], jac_point[1, v]], axis=0) * live for v in range(6)]
    spots = pt[...]
    eliminate(tracks, spots, table, rows_e)
    rows_c[...] = cams.astype(F32)
    rows_p[...] = spots.astype(F32)
    for v in range(12):
        rows_j[v] = jnp.concatenate([jac_cam[0, v], jac_cam[1, v]], axis=0)

    def block(q, carry):
        here = pl.ds(q, 1)
        hot_c = hot(rows_c[here], NCAM)
        hot_p = hot(rows_p[here], PTS)
        left = {}
        right = {}
        for r in range(2):
            hi_k, lo_k, hi_i, lo_i = [], [], [], []
            for k in range(6):
                hi, lo = split(rows_j[6 * r + k, here])
                hi_k.append(spread(hi, hot_p))
                lo_k.append(spread(lo, hot_p))
            for i in range(3):
                hi, lo = split(rows_e[3 * r + i, here])
                hi_i.append(spread(hi, hot_c))
                lo_i.append(spread(lo, hot_c))
            left[r] = (jnp.concatenate(hi_k, axis=0), jnp.concatenate(lo_k, axis=0))
            right[r] = (jnp.concatenate(hi_i, axis=0), jnp.concatenate(lo_i, axis=0))
        lhs = jnp.concatenate([left[0][0], left[1][0], left[0][1], left[1][1], left[0][0], left[1][0]], axis=1)
        rhs = jnp.concatenate([right[0][0], right[1][0], right[0][0], right[1][0], right[0][1], right[1][1]], axis=1)
        relayout(lax.dot_general(lhs, rhs, NT, preferred_element_type=F32), place(turned, 0, q))
        return carry

    lax.fori_loop(0, Q, block, 0, unroll=32)


def band_turned(payload, table, rows, turned, base):
    rows_e, rows_j, rows_c, rows_p = rows
    spots = payload[25].astype(F32)
    tracks = [payload[12 + v].astype(F32) + payload[18 + v].astype(F32) for v in range(6)]
    eliminate(tracks, spots.astype(jnp.int32), table, rows_e)
    rows_c[...] = payload[24].astype(F32)
    rows_p[...] = spots
    for v in range(12):
        rows_j[v] = payload[v].astype(F32)

    def block(q, carry):
        here = pl.ds(q, 1)
        hot_c = hot(rows_c[here], NCAM)
        hot_p = hot(rows_p[here], PTS)
        left = []
        right = []
        for r in range(2):
            left.append(jnp.concatenate([spread(rows_j[6 * r + k, here], hot_p) for k in range(6)], axis=0))
            cols = [spread(rows_e[3 * r + i, here], hot_c) for i in range(3)]
            right.append(jnp.concatenate(cols, axis=0))
        tile = lax.dot_general(
            jnp.concatenate(left, axis=1), jnp.concatenate(right, axis=1), NT, preferred_element_type=F32
        )
        relayout(tile, place(turned, base, q))
        return carry

    lax.fori_loop(0, Q, block, 0, unroll=32)


def fetch(refs, sems, start=0):
    return [pltpu.make_async_copy(x, y, sems.at[start + n]) for n, (x, y) in enumerate(refs)]


def show(ids, plan, loading, panel, order, turned, product, shown, out, sems):
    def place_out(p, j):
        step, cross = plan[p][2][j]
        there = lax.rem(ids[0] // 2 + step, 8)
        core = lax.rem(ids[0] + cross, 2)
        target = out.at[:, pl.ds(pl.multiple_of(there * (2 * ROWS) + ROWS * core, 128), ROWS)]
        return pltpu.make_async_copy(shown.at[p % 2, j], target, sems.at[p % 2, j])

    for p in range(len(plan)):
        for copy in loading[p]:
            copy.wait()
        product[...] = jnp.dot(panel[...], turned[p], preferred_element_type=F32)
        for j in range(2):
            if p >= 2:
                place_out(p - 2, j).wait()
            got = product[:, ROWS * j : ROWS * (j + 1)]
            hi = got.astype(BF16)
            lo = (got - hi.astype(F32)).astype(BF16)
            both = jnp.concatenate([hi, lo], axis=1)
            shown[p % 2, j] = lax.dot_general(both, order[...], NT, preferred_element_type=F32)
            place_out(p, j).start()
    for p in range(max(0, len(plan) - 2), len(plan)):
        for j in range(2):
            place_out(p, j).wait()


def own_panel(
    ids, cam, pt, jac_cam, jac_point, sum_mine, sum_other, order, up, down,
    out, panel_out, kept, table,
    rows_e, rows_j, rows_c, rows_p, turned, pair, product, panel, shown, sems, keep,
):
    rows = (rows_e, rows_j, rows_c, rows_p)
    core = lax.rem(ids[0], 2)
    near, far = invert(sum_mine[...]), invert(sum_other[...])
    for e in range(6):
        pieces = []
        for half in (jnp.where(core == 0, near[e], far[e]), jnp.where(core == 0, far[e], near[e])):
            for g in range(4):
                pieces.append(jnp.broadcast_to(half[g : g + 1], (4, 128)))
        table[e] = jnp.concatenate(pieces, axis=0)
    own_turned(cam, pt, jac_cam, jac_point, table, rows, turned)
    saved = fetch([(turned, kept.at[0]), (panel, panel_out)], keep)
    saved[0].start()
    panel[...] = lax.dot_general(
        order[:, :ROWS], turned[...], NT, preferred_element_type=F32
    ).astype(BF16)
    saved[1].start()
    for j, payload in enumerate((up, down)):
        band_turned(payload, table, rows, pair.at[0], ROWS * j)
        saved += fetch([(pair.at[0, :, ROWS * j : ROWS * (j + 1)], kept.at[1 + j])], keep, 2 + j)
        saved[-1].start()
    plan = (("build", (0, 1), ((7, 0), (1, 0))),)
    show(ids, plan, [[]], panel, order, pair, product, shown, out, sems)
    for copy in saved:
        copy.wait()


def tiles_kernel(plan, counts, first, *refs):
    builds, loads, groups = counts
    refs = list(refs)
    ids = refs.pop(0)
    payloads = [refs.pop(0) for _ in range(builds)]
    table, order, panel_in = (refs.pop(0) for _ in range(3))
    given = [refs.pop(0) for _ in range(loads)]
    if not first:
        refs.pop(0)
    out = refs.pop(0)
    kept = [refs.pop(0) for _ in range(groups)]
    rows_e, rows_j, rows_c, rows_p, turned, product, panel, shown, sems, keep = refs
    rows = (rows_e, rows_j, rows_c, rows_p)
    loading = [[] for _ in plan]
    semaphore = 1
    for p, (kind, sources, _) in enumerate(plan):
        if kind == "halves":
            parts = [given[n] if part is None else given[n].at[part] for n, part in sources]
            loading[p] = [
                pltpu.make_async_copy(parts[j], turned.at[p, :, ROWS * j : ROWS * (j + 1)], keep.at[semaphore + j])
                for j in range(2)
            ]
        semaphore += len(loading[p])
    fetched = pltpu.make_async_copy(panel_in, panel, keep.at[0])
    fetched.start()
    for copy in sum(loading, []):
        copy.start()
    leaving = []
    for p, (kind, sources, _) in enumerate(plan):
        if kind == "build":
            for j in range(2):
                band_turned(payloads[sources[j]], table, rows, turned.at[p], ROWS * j)
                if p < groups:
                    done = turned.at[p, :, ROWS * j : ROWS * (j + 1)]
                    leaving.append(pltpu.make_async_copy(done, kept[p].at[j], keep.at[semaphore + 2 * p + j]))
                    leaving[-1].start()
    fetched.wait()

    show(ids, plan, loading, panel, order, turned, product, shown, out, sems)
    for copy in leaving:
        copy.wait()


def row_scratch():
    return [
        pltpu.VMEM((6, Q, 128), F32),
        pltpu.VMEM((12, Q, 128), F32),
        pltpu.VMEM((Q, 128), F32),
        pltpu.VMEM((Q, 128), F32),
    ]


RESULT = jax.ShapeDtypeStruct((ROWS, NBLK * ROWS), F32)
PANEL = jax.ShapeDtypeStruct((ROWS, DEPTH), BF16)
PAIR = jax.ShapeDtypeStruct((2, DEPTH, ROWS), BF16)


def tiles(ids, plan, payloads, given, groups, table, order, panel, out):
    first = out is None
    builds, loads = len(payloads), len(given)
    specs = [smem()] + [vmem()] * (builds + 2) + [anywhere()] * (1 + loads)
    args = [ids, *payloads, table, order, panel, *given]
    aliases = {}
    if not first:
        specs.append(anywhere())
        aliases = {len(args): 0}
        args.append(out)
    pair = PAIR
    return pl.pallas_call(
        functools.partial(tiles_kernel, plan, (builds, loads, groups), first),
        out_shape=(RESULT,) + (pair,) * groups,
        in_specs=specs,
        out_specs=(anywhere(),) * (1 + groups),
        input_output_aliases=aliases,
        scratch_shapes=row_scratch()
        + [
            pltpu.VMEM((len(plan), DEPTH, 2 * ROWS), BF16),
            pltpu.VMEM((ROWS, 2 * ROWS), F32),
            pltpu.VMEM((ROWS, DEPTH), BF16),
            pltpu.VMEM((2, 2, ROWS, ROWS), F32),
            pltpu.SemaphoreType.DMA((2, 2)),
            pltpu.SemaphoreType.DMA((9,)),
        ],
        compiler_params=params(),
        cost_estimate=cost(12),
    )(*args)


def order_matrix():
    row = np.arange(ROWS)
    one = (row[:, None] // 6 == row[None] % NCAM) & (row[:, None] % 6 == row[None] // NCAM)
    return np.concatenate([one, one], axis=1).astype(np.float32)


def body(cam_index, point_index, jac_cam, jac_point, point_damping):
    cam = cam_index.reshape(Q, 128)
    pt = point_index.reshape(Q, 128)
    jac_cam = jac_cam.reshape(2, 12, NBLK, 128)
    jac_point = jac_point.reshape(2, 6, NBLK, 128)
    damping = point_damping.reshape(1, PTS)
    ids = lax.axis_index("blk").astype(jnp.int32).reshape(1)
    order = jnp.asarray(order_matrix(), BF16)
    shape = jax.ShapeDtypeStruct
    payload, mine, other = pl.pallas_call(
        prepare,
        out_shape=(shape((VALS, Q, 128), BF16), shape((24, 128), F32), shape((24, 128), F32)),
        in_specs=[smem()] + [vmem()] * 5,
        out_specs=(vmem(),) * 3,
        scratch_shapes=[pltpu.VMEM((Q, 8, 128), F32)],
        compiler_params=params(),
    )(ids, cam, pt, jac_cam, jac_point, damping)

    def moved(x, by, cross):
        pairs = [(n, (n + 2 * by) % NBLK ^ cross) for n in range(NBLK)]
        return lax.ppermute(x, "blk", pairs)

    parts = mine + moved(other, 0, 1)
    up1, down1 = moved(payload, 1, 0), moved(payload, -1, 0)
    groups = []
    for s in range(16):
        after = (s + 1) % 16
        groups.append([s * NBLK + 2 * z + 1 for z in range(8)] + [after * NBLK + 2 * z for z in range(8)])
    parts = lax.all_to_all(
        jnp.broadcast_to(parts[None], (16, 24, 128)),
        ("cam", "blk"),
        split_axis=0,
        concat_axis=0,
        axis_index_groups=groups,
        tiled=True,
    )
    sum_mine = parts.sum(axis=0)
    sum_other = moved(sum_mine, 0, 1)
    up1, down1, _ = lax.optimization_barrier((up1, down1, sum_mine))
    sum_other = moved(sum_mine, 0, 1)
    up2, down2 = moved(up1, 1, 0), moved(down1, -1, 0)
    out, panel, made1, table = pl.pallas_call(
        own_panel,
        out_shape=(RESULT, PANEL, shape((3, DEPTH, ROWS), BF16), shape((6, Q, 128), F32)),
        in_specs=[smem()] + [vmem()] * 9,
        out_specs=(anywhere(),) * 3 + (vmem(),),
        scratch_shapes=row_scratch()
        + [
            pltpu.VMEM((DEPTH, ROWS), BF16),
            pltpu.VMEM((1, DEPTH, 2 * ROWS), BF16),
            pltpu.VMEM((ROWS, 2 * ROWS), F32),
            pltpu.VMEM(PANEL.shape, BF16),
            pltpu.VMEM((2, 2, ROWS, ROWS), F32),
            pltpu.SemaphoreType.DMA((2, 2)),
            pltpu.SemaphoreType.DMA((4,)),
        ],
        compiler_params=params(),
        cost_estimate=cost(12),
    )(ids, cam, pt, jac_cam, jac_point, sum_mine, sum_other, order, up1, down1)
    up2, down2, made1 = lax.optimization_barrier((up2, down2, made1))
    mates1 = moved(made1, 0, 1)
    up3, down3 = moved(up2, 1, 0), moved(down2, -1, 0)
    plan = (("build", (0, 1), ((6, 0), (2, 0))),)
    out, made2 = tiles(ids, plan, [up2, down2], [], 1, table, order, panel, out)
    up3, down3, out = lax.optimization_barrier((up3, down3, out))
    up4, cross4 = moved(up3, 1, 0), moved(up3, 1, 1)
    mate_up, mate_down = moved(up3, 0, 1), moved(down3, 0, 1)
    mate_up, mate_down, made2, out = lax.optimization_barrier((mate_up, mate_down, made2, out))
    mates2 = moved(made2, 0, 1)
    plan = (("build", (0, 1), ((5, 0), (3, 0))), ("halves", ((0, 0), (1, 0)), ((0, 0), (0, 1))))
    out = tiles(ids, plan, [up3, down3], [made1, mates1], 0, table, order, panel, out)[0]
    plan = (
        ("build", (0, 1), ((5, 1), (3, 1))),
        ("build", (2, 3), ((4, 0), (4, 1))),
        ("halves", ((0, 1), (0, 2)), ((7, 1), (1, 1))),
        ("halves", ((1, 0), (1, 1)), ((6, 1), (2, 1))),
    )
    payloads = [mate_up, mate_down, up4, cross4]
    return tiles(ids, plan, payloads, [mates1, mates2], 0, table, order, panel, out)[0]


def solution(mesh):
    return jax.shard_map(
        body,
        mesh=mesh,
        in_specs=(
            P("cam", "blk", None, None, None),
            P("cam", "blk", None, None, None),
            P("cam", "blk", None, None, None, None),
            P("cam", "blk", None, None, None, None),
            P("cam", "blk", None),
        ),
        out_specs=P(("cam", "blk"), None),
        check_vma=False,
    )
```

```python
import functools

import jax
import jax.numpy as jnp
import numpy as np
from jax import lax
from jax.experimental import pallas as pl
from jax.experimental.pallas import tpu as pltpu
from jax.sharding import PartitionSpec as P

F32 = jnp.float32
BF16 = jnp.bfloat16
NT = (((1,), (1,)), ((), ()))
NCAM = 64
NBLK = 16
PTS = 32
Q = 2 * NBLK
ROWS = NCAM * 6
DEPTH = 3 * PTS * Q
VALS = 26
PAIRS = ((0, 0), (0, 1), (0, 2), (1, 1), (1, 2), (2, 2))


def vmem():
    return pl.BlockSpec(memory_space=pltpu.VMEM)


def anywhere():
    return pl.BlockSpec(memory_space=pl.ANY)


def smem():
    return pl.BlockSpec(memory_space=pltpu.SMEM)


def params():
    return pltpu.CompilerParams(vmem_limit_bytes=62 * 2**20)


def cost(us):
    return pl.CostEstimate(flops=int(us * 1.2e9), transcendentals=0, bytes_accessed=int(us * 3e6))


def split(x):
    hi = x.astype(BF16).astype(F32)
    return hi, x - hi


def prepare(ids, cam, pt, jac_cam, jac_point, damping, payload, mine, other, prods):
    core = lax.rem(ids[0], 2)
    lane = lax.broadcasted_iota(jnp.int32, (8, 128), 1)
    entry = lax.broadcasted_iota(jnp.int32, (8, 128), 0)
    diag = (entry == 0) | (entry == 3) | (entry == 5)
    damp = jnp.broadcast_to(jnp.concatenate([damping[...]] * 4, axis=1), (8, 128))
    damp = jnp.where(diag & (lane // PTS == lax.rem(ids[0], 4)), damp, 0.0)
    rows128 = lax.broadcasted_iota(jnp.int32, (128, 128), 0)
    totals = []
    for p in range(2):
        span = pl.ds(p * NBLK, NBLK)
        cams = cam[span]
        live = (cams < NCAM).astype(F32)
        payload[24, span] = cams.astype(F32).astype(BF16)
        payload[25, span] = pt[span].astype(F32).astype(BF16)
        for v in range(12):
            payload[v, span] = jac_cam[p, v].astype(BF16)
        tracks = [jac_point[p, v] * live for v in range(6)]
        for v in range(6):
            hi, lo = split(tracks[v])
            payload[12 + v, span] = hi.astype(BF16)
            payload[18 + v, span] = lo.astype(BF16)
        for e, (i, j) in enumerate(PAIRS):
            prods[span, e] = tracks[i] * tracks[j] + tracks[3 + i] * tracks[3 + j]
        prods[span, 6] = jnp.zeros((NBLK, 128), F32)
        prods[span, 7] = jnp.zeros((NBLK, 128), F32)
        for g in range(4):
            left = []
            right = []
            for t in range(4):
                q = p * NBLK + 4 * g + t
                hi, rest = split(prods[q])
                mid, low = split(rest)
                left.append(jnp.concatenate([hi, mid, low, jnp.zeros((8, 128), F32)], axis=0).astype(BF16))
                spot = jnp.broadcast_to(pt[pl.ds(q, 1)], (128, 128)) + PTS * t
                right.append(jnp.where(spot == rows128, 1.0, 0.0).astype(BF16))
            got = lax.dot_general(
                jnp.concatenate(left, axis=1), jnp.concatenate(right, axis=1), NT, preferred_element_type=F32
            )
            total = got[0:8] + got[8:16] + got[16:24]
            if p == 0:
                total = total + jnp.where(ids[0] // 4 == g, damp, 0.0)
            totals.append(total)
    for g in range(4):
        near = jnp.where(core == 0, totals[g], totals[4 + g])
        far = jnp.where(core == 0, totals[4 + g], totals[g])
        for e in range(6):
            mine[4 * e + g : 4 * e + g + 1] = near[e : e + 1]
            other[4 * e + g : 4 * e + g + 1] = far[e : e + 1]


def invert(total):
    sym = [total[4 * e : 4 * e + 4] for e in range(6)]
    root_first = jnp.sqrt(sym[0])
    low_second = sym[1] / root_first
    low_third = sym[2] / root_first
    root_second = jnp.sqrt(sym[3] - low_second * low_second)
    low_mixed = (sym[4] - low_third * low_second) / root_second
    root_third = jnp.sqrt(sym[5] - low_third * low_third - low_mixed * low_mixed)
    inv_first = 1.0 / root_first
    inv_second = 1.0 / root_second
    inv_third = 1.0 / root_third
    inv_lower = -inv_second * low_second * inv_first
    inv_mixed = -inv_third * low_mixed * inv_second
    inv_corner = -(inv_mixed * low_second + inv_third * low_third) * inv_first
    return (inv_first, inv_lower, inv_second, inv_corner, inv_mixed, inv_third)


def eliminate(tracks, spots, table, rows_out):
    offset = lax.rem(lax.broadcasted_iota(jnp.int32, (Q, 128), 0), 4) * PTS
    where = spots + offset
    looked = [jnp.take_along_axis(table[e], where, axis=1) for e in range(6)]
    for r in range(2):
        first, second, third = tracks[3 * r : 3 * r + 3]
        rows_out[3 * r] = first * looked[0]
        rows_out[3 * r + 1] = first * looked[1] + second * looked[2]
        rows_out[3 * r + 2] = first * looked[3] + second * looked[4] + third * looked[5]


def hot(spot, count):
    rows = lax.broadcasted_iota(jnp.int32, (count, 128), 0).astype(F32)
    return jnp.where(jnp.broadcast_to(spot, (count, 128)) == rows, 1.0, 0.0).astype(BF16)


def spread(row, mask):
    value = jnp.broadcast_to(row, (16, 128)).astype(BF16)
    return jnp.concatenate([value] * (mask.shape[0] // 16), axis=0) * mask


def relayout(tile, store):
    low = lax.broadcasted_iota(jnp.int32, (PTS, 128), 1) < NCAM
    for m in range(3):
        even = tile[64 * m : 64 * m + 32]
        odd = tile[64 * m + 32 : 64 * m + 64]
        even_rolled = pltpu.roll(even[:, :128], 64, axis=1)
        odd_rolled = pltpu.roll(odd[:, :128], 64, axis=1)
        last = jnp.concatenate([even[:, 128:], odd[:, 128:]], axis=1)
        store(0, m, jnp.where(low, even[:, :128], odd_rolled))
        store(1, m, jnp.where(low, even_rolled, odd[:, :128]))
        store(2, m, last)


def place(turned, base, q):
    def store(i, m, value):
        at = pl.multiple_of(q * 96 + 32 * i, 32)
        turned[base // 128 + m, pl.ds(at, 32)] = value.astype(BF16)

    return store


def own_turned(cam, pt, jac_cam, jac_point, table, rows, turned):
    rows_e, rows_j, rows_c, rows_p = rows
    cams = cam[...]
    live = (cams < NCAM).astype(F32)
    tracks = [jnp.concatenate([jac_point[0, v], jac_point[1, v]], axis=0) * live for v in range(6)]
    spots = pt[...]
    eliminate(tracks, spots, table, rows_e)
    rows_c[...] = cams.astype(F32)
    rows_p[...] = spots.astype(F32)
    for v in range(12):
        rows_j[v] = jnp.concatenate([jac_cam[0, v], jac_cam[1, v]], axis=0)

    def block(q, carry):
        here = pl.ds(q, 1)
        hot_c = hot(rows_c[here], NCAM)
        hot_p = hot(rows_p[here], PTS)
        left = {}
        right = {}
        for r in range(2):
            hi_k, lo_k, hi_i, lo_i = [], [], [], []
            for k in range(6):
                hi, lo = split(rows_j[6 * r + k, here])
                hi_k.append(spread(hi, hot_p))
                lo_k.append(spread(lo, hot_p))
            for i in range(3):
                hi, lo = split(rows_e[3 * r + i, here])
                hi_i.append(spread(hi, hot_c))
                lo_i.append(spread(lo, hot_c))
            left[r] = (jnp.concatenate(hi_k, axis=0), jnp.concatenate(lo_k, axis=0))
            right[r] = (jnp.concatenate(hi_i, axis=0), jnp.concatenate(lo_i, axis=0))
        lhs = jnp.concatenate([left[0][0], left[1][0], left[0][1], left[1][1], left[0][0], left[1][0]], axis=1)
        rhs = jnp.concatenate([right[0][0], right[1][0], right[0][0], right[1][0], right[0][1], right[1][1]], axis=1)
        relayout(lax.dot_general(lhs, rhs, NT, preferred_element_type=F32), place(turned, 0, q))
        return carry

    lax.fori_loop(0, Q, block, 0, unroll=32)


def band_turned(payload, table, rows, turned, base):
    rows_e, rows_j, rows_c, rows_p = rows
    spots = payload[25].astype(F32)
    tracks = [payload[12 + v].astype(F32) + payload[18 + v].astype(F32) for v in range(6)]
    eliminate(tracks, spots.astype(jnp.int32), table, rows_e)
    rows_c[...] = payload[24].astype(F32)
    rows_p[...] = spots
    for v in range(12):
        rows_j[v] = payload[v].astype(F32)

    def block(q, carry):
        here = pl.ds(q, 1)
        hot_c = hot(rows_c[here], NCAM)
        hot_p = hot(rows_p[here], PTS)
        left = []
        right = []
        for r in range(2):
            left.append(jnp.concatenate([spread(rows_j[6 * r + k, here], hot_p) for k in range(6)], axis=0))
            cols = [spread(rows_e[3 * r + i, here], hot_c) for i in range(3)]
            right.append(jnp.concatenate(cols, axis=0))
        tile = lax.dot_general(
            jnp.concatenate(left, axis=1), jnp.concatenate(right, axis=1), NT, preferred_element_type=F32
        )
        relayout(tile, place(turned, base, q))
        return carry

    lax.fori_loop(0, Q, block, 0, unroll=32)


def fetch(refs, sems, start=0):
    return [pltpu.make_async_copy(x, y, sems.at[start + n]) for n, (x, y) in enumerate(refs)]


def wide(ref, count):
    return jnp.concatenate([ref[n] for n in range(count)], axis=1)


def show(ids, plan, loading, panel, order, turned, product, shown, out, sems):
    def place_out(p, j):
        step, cross = plan[p][2][j]
        there = lax.rem(ids[0] // 2 + step, 8)
        core = lax.rem(ids[0] + cross, 2)
        target = out.at[:, pl.ds(pl.multiple_of(there * (2 * ROWS) + ROWS * core, 128), ROWS)]
        return pltpu.make_async_copy(shown.at[p % 2, j], target, sems.at[p % 2, j])

    for p in range(len(plan)):
        for copy in loading[p]:
            copy.wait()
        product[...] = jnp.dot(wide(panel, 24), wide(turned.at[p], 6), preferred_element_type=F32)
        for j in range(2):
            if p >= 2:
                place_out(p - 2, j).wait()
            got = product[:, ROWS * j : ROWS * (j + 1)]
            hi = got.astype(BF16)
            lo = (got - hi.astype(F32)).astype(BF16)
            both = jnp.concatenate([hi, lo], axis=1)
            shown[p % 2, j] = lax.dot_general(both, order[...], NT, preferred_element_type=F32)
            place_out(p, j).start()
    for p in range(max(0, len(plan) - 2), len(plan)):
        for j in range(2):
            place_out(p, j).wait()


def own_panel(
    ids, cam, pt, jac_cam, jac_point, sum_mine, sum_other, order, up, down,
    out, panel_out, kept, table,
    rows_e, rows_j, rows_c, rows_p, turned, pair, product, panel, shown, sems, keep,
):
    rows = (rows_e, rows_j, rows_c, rows_p)
    core = lax.rem(ids[0], 2)
    near, far = invert(sum_mine[...]), invert(sum_other[...])
    for e in range(6):
        pieces = []
        for half in (jnp.where(core == 0, near[e], far[e]), jnp.where(core == 0, far[e], near[e])):
            for g in range(4):
                pieces.append(jnp.broadcast_to(half[g : g + 1], (4, 128)))
        table[e] = jnp.concatenate(pieces, axis=0)
    own_turned(cam, pt, jac_cam, jac_point, table, rows, turned)
    saved = fetch([(turned, kept.at[0]), (panel, panel_out)], keep)
    saved[0].start()
    left = lax.dot_general(order[:, :ROWS], wide(turned, 3), NT, preferred_element_type=F32).astype(BF16)
    for n in range(24):
        panel[n] = left[:, 128 * n : 128 * n + 128]
    saved[1].start()
    for j, payload in enumerate((up, down)):
        band_turned(payload, table, rows, pair.at[0], ROWS * j)
        saved += fetch([(pair.at[0, pl.ds(3 * j, 3)], kept.at[1 + j])], keep, 2 + j)
        saved[-1].start()
    plan = (("build", (0, 1), ((7, 0), (1, 0))),)
    show(ids, plan, [[]], panel, order, pair, product, shown, out, sems)
    for copy in saved:
        copy.wait()


def tiles_kernel(plan, counts, first, *refs):
    builds, loads, groups = counts
    refs = list(refs)
    ids = refs.pop(0)
    payloads = [refs.pop(0) for _ in range(builds)]
    table, order, panel_in = (refs.pop(0) for _ in range(3))
    given = [refs.pop(0) for _ in range(loads)]
    if not first:
        refs.pop(0)
    out = refs.pop(0)
    kept = [refs.pop(0) for _ in range(groups)]
    rows_e, rows_j, rows_c, rows_p, turned, product, panel, shown, sems, keep = refs
    rows = (rows_e, rows_j, rows_c, rows_p)
    loading = [[] for _ in plan]
    semaphore = 1
    for p, (kind, sources, _) in enumerate(plan):
        if kind == "halves":
            parts = [given[n] if part is None else given[n].at[part] for n, part in sources]
            loading[p] = [
                pltpu.make_async_copy(parts[j], turned.at[p, pl.ds(3 * j, 3)], keep.at[semaphore + j])
                for j in range(2)
            ]
        semaphore += len(loading[p])
    fetched = pltpu.make_async_copy(panel_in, panel, keep.at[0])
    fetched.start()
    for copy in sum(loading, []):
        copy.start()
    leaving = []
    for p, (kind, sources, _) in enumerate(plan):
        if kind == "build":
            for j in range(2):
                band_turned(payloads[sources[j]], table, rows, turned.at[p], ROWS * j)
                if p < groups:
                    done = turned.at[p, pl.ds(3 * j, 3)]
                    leaving.append(pltpu.make_async_copy(done, kept[p].at[j], keep.at[semaphore + 2 * p + j]))
                    leaving[-1].start()
    fetched.wait()

    show(ids, plan, loading, panel, order, turned, product, shown, out, sems)
    for copy in leaving:
        copy.wait()


def row_scratch():
    return [
        pltpu.VMEM((6, Q, 128), F32),
        pltpu.VMEM((12, Q, 128), F32),
        pltpu.VMEM((Q, 128), F32),
        pltpu.VMEM((Q, 128), F32),
    ]


RESULT = jax.ShapeDtypeStruct((ROWS, NBLK * ROWS), F32)
PANEL = jax.ShapeDtypeStruct((24, ROWS, 128), BF16)
PAIR = jax.ShapeDtypeStruct((2, 3, DEPTH, 128), BF16)


def tiles(ids, plan, payloads, given, groups, table, order, panel, out):
    first = out is None
    builds, loads = len(payloads), len(given)
    specs = [smem()] + [vmem()] * (builds + 2) + [anywhere()] * (1 + loads)
    args = [ids, *payloads, table, order, panel, *given]
    aliases = {}
    if not first:
        specs.append(anywhere())
        aliases = {len(args): 0}
        args.append(out)
    pair = PAIR
    return pl.pallas_call(
        functools.partial(tiles_kernel, plan, (builds, loads, groups), first),
        out_shape=(RESULT,) + (pair,) * groups,
        in_specs=specs,
        out_specs=(anywhere(),) * (1 + groups),
        input_output_aliases=aliases,
        scratch_shapes=row_scratch()
        + [
            pltpu.VMEM((len(plan), 6, DEPTH, 128), BF16),
            pltpu.VMEM((ROWS, 2 * ROWS), F32),
            pltpu.VMEM(PANEL.shape, BF16),
            pltpu.VMEM((2, 2, ROWS, ROWS), F32),
            pltpu.SemaphoreType.DMA((2, 2)),
            pltpu.SemaphoreType.DMA((9,)),
        ],
        compiler_params=params(),
        cost_estimate=cost(12),
    )(*args)


def order_matrix():
    row = np.arange(ROWS)
    one = (row[:, None] // 6 == row[None] % NCAM) & (row[:, None] % 6 == row[None] // NCAM)
    return np.concatenate([one, one], axis=1).astype(np.float32)


def body(cam_index, point_index, jac_cam, jac_point, point_damping):
    cam = cam_index.reshape(Q, 128)
    pt = point_index.reshape(Q, 128)
    jac_cam = jac_cam.reshape(2, 12, NBLK, 128)
    jac_point = jac_point.reshape(2, 6, NBLK, 128)
    damping = point_damping.reshape(1, PTS)
    ids = lax.axis_index("blk").astype(jnp.int32).reshape(1)
    order = jnp.asarray(order_matrix(), BF16)
    shape = jax.ShapeDtypeStruct
    payload, mine, other = pl.pallas_call(
        prepare,
        out_shape=(shape((VALS, Q, 128), BF16), shape((24, 128), F32), shape((24, 128), F32)),
        in_specs=[smem()] + [vmem()] * 5,
        out_specs=(vmem(),) * 3,
        scratch_shapes=[pltpu.VMEM((Q, 8, 128), F32)],
        compiler_params=params(),
    )(ids, cam, pt, jac_cam, jac_point, damping)

    def moved(x, by, cross):
        pairs = [(n, (n + 2 * by) % NBLK ^ cross) for n in range(NBLK)]
        return lax.ppermute(x, "blk", pairs)

    parts = mine + moved(other, 0, 1)
    up1, down1 = moved(payload, 1, 0), moved(payload, -1, 0)
    groups = []
    for s in range(16):
        after = (s + 1) % 16
        groups.append([s * NBLK + 2 * z + 1 for z in range(8)] + [after * NBLK + 2 * z for z in range(8)])
    parts = lax.all_to_all(
        jnp.broadcast_to(parts[None], (16, 24, 128)),
        ("cam", "blk"),
        split_axis=0,
        concat_axis=0,
        axis_index_groups=groups,
        tiled=True,
    )
    sum_mine = parts.sum(axis=0)
    sum_other = moved(sum_mine, 0, 1)
    up1, down1, _ = lax.optimization_barrier((up1, down1, sum_mine))
    sum_other = moved(sum_mine, 0, 1)
    up2, down2 = moved(up1, 1, 0), moved(down1, -1, 0)
    out, panel, made1, table = pl.pallas_call(
        own_panel,
        out_shape=(RESULT, PANEL, shape((3, 3, DEPTH, 128), BF16), shape((6, Q, 128), F32)),
        in_specs=[smem()] + [vmem()] * 9,
        out_specs=(anywhere(),) * 3 + (vmem(),),
        scratch_shapes=row_scratch()
        + [
            pltpu.VMEM((3, DEPTH, 128), BF16),
            pltpu.VMEM((1, 6, DEPTH, 128), BF16),
            pltpu.VMEM((ROWS, 2 * ROWS), F32),
            pltpu.VMEM(PANEL.shape, BF16),
            pltpu.VMEM((2, 2, ROWS, ROWS), F32),
            pltpu.SemaphoreType.DMA((2, 2)),
            pltpu.SemaphoreType.DMA((4,)),
        ],
        compiler_params=params(),
        cost_estimate=cost(12),
    )(ids, cam, pt, jac_cam, jac_point, sum_mine, sum_other, order, up1, down1)
    up2, down2, made1 = lax.optimization_barrier((up2, down2, made1))
    mates1 = moved(made1, 0, 1)
    up3, down3 = moved(up2, 1, 0), moved(down2, -1, 0)
    plan = (("build", (0, 1), ((6, 0), (2, 0))),)
    out, made2 = tiles(ids, plan, [up2, down2], [], 1, table, order, panel, out)
    up3, down3, out = lax.optimization_barrier((up3, down3, out))
    up4, cross4 = moved(up3, 1, 0), moved(up3, 1, 1)
    mate_up, mate_down = moved(up3, 0, 1), moved(down3, 0, 1)
    mate_up, mate_down, made2, out = lax.optimization_barrier((mate_up, mate_down, made2, out))
    mates2 = moved(made2, 0, 1)
    plan = (("build", (0, 1), ((5, 0), (3, 0))), ("halves", ((0, 0), (1, 0)), ((0, 0), (0, 1))))
    out = tiles(ids, plan, [up3, down3], [made1, mates1], 0, table, order, panel, out)[0]
    plan = (
        ("build", (0, 1), ((5, 1), (3, 1))),
        ("build", (2, 3), ((4, 0), (4, 1))),
        ("halves", ((0, 1), (0, 2)), ((7, 1), (1, 1))),
        ("halves", ((1, 0), (1, 1)), ((6, 1), (2, 1))),
    )
    payloads = [mate_up, mate_down, up4, cross4]
    return tiles(ids, plan, payloads, [mates1, mates2], 0, table, order, panel, out)[0]


def solution(mesh):
    return jax.shard_map(
        body,
        mesh=mesh,
        in_specs=(
            P("cam", "blk", None, None, None),
            P("cam", "blk", None, None, None),
            P("cam", "blk", None, None, None, None),
            P("cam", "blk", None, None, None, None),
            P("cam", "blk", None),
        ),
        out_specs=P(("cam", "blk"), None),
        check_vma=False,
    )
```
